32 devices in a mesh: ctx: 4 (over x, core), exp: 8 (over z, y).
Axes of the slice: x: 2, y: 2, z: 4, core: 2. Of those that a mesh axis runs over, the one named last changes fastest.
Arguments:
- tokens: bfloat16 [8, 512, 1024], P('exp', 'ctx'), may hold values from -300 to 300, as said below
- expert_ids: int32 [8, 512, 2], P('exp', 'ctx'), may hold values from 0 to 7, all different within a row; in each aligned block of 128 rows (0 to 127, 128 to 255, ..., all dimensions but the last counted through in order) at most 48 rows name the same one
- attn_gain: float32 [1024], replicated, may hold values from 0.1 to 1.9
- w_query: bfloat16 [1024, 1024], P('exp'), may hold values from -0.1875 to 0.1875
- w_kv: bfloat16 [1024, 256], P('exp'), may hold values from -0.1875 to 0.1875
- w_out: bfloat16 [1024, 1024], P('exp'), may hold values from -0.1875 to 0.1875
- moe_gain: float32 [1024], replicated, may hold values from 0.1 to 1.9
- router: bfloat16 [1024, 8], replicated, may hold values from -0.375 to 0.375
- w_gate: bfloat16 [8, 1024, 4096], P('exp', None, 'ctx'), may hold values from -0.1875 to 0.1875
- w_up: bfloat16 [8, 1024, 4096], P('exp', None, 'ctx'), may hold values from -0.1875 to 0.1875
- w_down: bfloat16 [8, 4096, 1024], P('exp', 'ctx'), may hold values from -0.1875 to 0.1875
Outputs:
- attention_out: bfloat16 [8, 512, 1024], P('exp', 'ctx')
- expert_mix: bfloat16 [8, 512, 1024], P('exp', 'ctx')
The draws below stay inside these ranges and needn't reach their ends.
Inputs may be any that keep to these rules, and one draw needn't show every extreme that they name: `expert_ids`: each row names 2 different experts. In the rows of one device (aligned blocks of 128 positions) no expert is named more than 48 times, a bound that some block reaches in every draw. `tokens`: each token and each feature carries its own scale.
All inputs are finite; a program needn't handle non-finite values.
Results may differ from the reference program's by a relative error of at most 0.018.
Values may be sent and summed in bfloat16 or wider, within the bound.
No kernel may reach another device: no remote copies, remote signals or barrier semaphores. Data moves between devices by JAX's collectives and lax.ppermute only.
A program may use at most 128 MiB of HBM per device.

```python
import math
import jax
import jax.numpy as jnp
import numpy as np
from jax import lax

D = 1024
HEADS = 8
HD = 128
EFF = 4096
TOP = 2
TOK_DEV = 128
EXPERTS = 8
LENGTH = 512
DOMAINS = 8
CAP = 48
N_CTX = 4


def draw_tokens(key, part):
    key_base, key_rows, key_cols = jax.random.split(key, 3)
    shape = (DOMAINS, LENGTH, D)
    base = jax.random.normal(key_base, shape, jnp.float32)
    row_scale = jnp.exp(jax.random.uniform(key_rows, (DOMAINS, LENGTH, 1), jnp.float32, 0.0, math.log(10.0)))
    col_scale = jnp.exp(jax.random.uniform(key_cols, (1, 1, D), jnp.float32, -1.2, 1.2))
    return (base * row_scale * col_scale).astype(jnp.bfloat16)


def steps_of(stream_key, dims, pieces, smallest, top_value):
    loudness = 1.0
    for axis_at, parts in pieces:
        steps = jax.random.uniform(jax.random.fold_in(jax.random.fold_in(stream_key, 6), axis_at), (parts,), jnp.float32, smallest / len(pieces), top_value / len(pieces))
        loudness = loudness * jnp.repeat(jnp.exp(steps), dims[axis_at] // parts).reshape((-1,) + (1,) * (len(dims) - 1 - axis_at))
    return loudness


def shared_out(rng, own, number, rows, count, top, reach, skew):
    order = jax.random.permutation(rng, count)
    crowded, ordinary = shares(count, rows * top, reach, skew, True), shares(count, rows * top, reach, skew, False)
    places = jnp.arange(count)

    def named(sizes, offset_by):
        used = int((sizes > 0).sum())
        fixed = max(1, used // 4)
        moved = fixed + (places - fixed + offset_by * (used - fixed)) % max(1, count - fixed)
        return jnp.zeros((count,), jnp.int32).at[order[jnp.where(places < fixed, places, moved)]].set(jnp.asarray(sizes, jnp.int32))

    sizes = jnp.where(number % 4 == 0, named(crowded, number // 4), named(ordinary, number - number // 4 - 1))
    mixed = jax.random.permutation(jax.random.fold_in(own, 3), count)
    source_of, taker = mixed[0:count // 2 * 2:2], mixed[1:count // 2 * 2:2]
    margin = jnp.minimum(sizes[source_of] - 1, reach - sizes[taker]) // 2
    margin = jnp.where((source_of == order[0]) | (taker == order[0]) | (sizes[taker] == 0), 0, jnp.maximum(margin, 0))
    moved = jax.random.randint(jax.random.fold_in(own, 4), (count // 2,), 0, 1 << 20) % (margin + 1)
    sizes = sizes.at[source_of].add(-moved).at[taker].add(moved)
    labels = jnp.searchsorted(jnp.cumsum(sizes), jnp.arange(rows * top), side="right").astype(jnp.int32)
    table = labels.reshape(top, rows).T
    table = table[jax.random.permutation(jax.random.fold_in(own, 1), rows)]
    offset_by = jax.random.randint(jax.random.fold_in(own, 2), (rows, 1), 0, top)
    return jnp.take_along_axis(table, (jnp.arange(top)[None, :] + offset_by) % top, axis=1)


def shares(count, total, bound, skew, full):
    loads = [(1 << 20) // math.isqrt(grade ** skew) + 1 for grade in range(1, count + 1)]
    largest = bound if full else min(bound, max(-(-total // count), total * loads[0] // sum(loads)))
    least = 1 if total - largest >= count - 1 else 0
    given, surplus = [largest] + [least] * (count - 1), total - largest - least * (count - 1)
    while surplus > 0:
        candidates = [i for i in range(1, count) if given[i] < largest] or [i for i in range(1, count) if given[i] < bound]
        whole, remaining = sum([loads[i] for i in candidates]), surplus
        for i in candidates:
            extra = min(bound - given[i], max(1, remaining * loads[i] // whole), surplus)
            given[i] = given[i] + extra
            surplus = surplus - extra
    return np.array(given)


def centred(rng, extent, deviation, limit, cuts=(), kind=jnp.bfloat16):
    array = jax.random.normal(rng, extent, jnp.float32) * deviation
    if len(cuts) > 0:
        array = steps_of(rng, extent, cuts, -0.22, 0.18) * array
    return jnp.clip(array, min=-limit, max=limit).astype(kind)


def setup_inputs(seed: int = 0) -> dict:
    splits = jax.random.split(jax.random.key(seed), 12)
    tokens = draw_tokens(jax.random.fold_in(splits[11], 71), 0)
    expert_ids_keys = jax.random.split(jax.random.fold_in(splits[1], 1), DOMAINS * LENGTH // TOK_DEV)
    expert_ids_turns = jax.random.permutation(jax.random.fold_in(splits[1], 3), DOMAINS * LENGTH // TOK_DEV)
    expert_ids = jax.vmap(lambda own, number: shared_out(jax.random.fold_in(splits[1], 2), own, number, TOK_DEV, EXPERTS, TOP, CAP, 2))(expert_ids_keys, expert_ids_turns).reshape((DOMAINS, LENGTH, TOP))
    attn_gain = jnp.clip(1.0 + 0.18 * jax.random.normal(splits[2], (D,), jnp.float32), 0.1, 1.9)
    w_query = centred(splits[3], (D, HEADS * HD), D ** -0.5, 0.1875, ((0, 8),))
    w_kv = centred(splits[4], (D, 2 * HD), D ** -0.5, 0.1875, ((0, 8),))
    w_out = centred(splits[5], (HEADS * HD, D), (HEADS * HD) ** -0.5, 0.1875, ((0, 8),))
    moe_gain = jnp.clip(1.0 + 0.18 * jax.random.normal(splits[6], (D,), jnp.float32), 0.1, 1.9)
    router = centred(splits[7], (D, EXPERTS), (D // 4) ** -0.5, 0.375)
    w_gate = centred(splits[8], (EXPERTS, D, EFF), D ** -0.5, 0.1875, ((0, 8), (2, 4)))
    w_up = centred(splits[9], (EXPERTS, D, EFF), D ** -0.5, 0.1875, ((0, 8), (2, 4)))
    w_down = centred(splits[10], (EXPERTS, EFF, D), (EFF // 4) ** -0.5, 0.1875, ((0, 8), (1, 4)))
    return dict(tokens=tokens, expert_ids=expert_ids, attn_gain=attn_gain, w_query=w_query, w_kv=w_kv, w_out=w_out, moe_gain=moe_gain, router=router, w_gate=w_gate, w_up=w_up, w_down=w_down)


epsilon = 1e-06

def rms_scaled(values):
    return values * lax.rsqrt(lax.optimization_barrier(jnp.mean(values * values, axis=-1, keepdims=True)) + epsilon)

def reference(tokens, expert_ids, attn_gain, w_query, w_kv, w_out, moe_gain, router, w_gate, w_up, w_down):
    floats = tokens.astype(jnp.float32)
    attn_in = (rms_scaled(floats) * attn_gain).astype(jnp.bfloat16)
    score_scale = HD ** (-0.5)

    def attend(sequence):
        queries = jnp.dot(sequence, w_query, preferred_element_type=jnp.float32).reshape(LENGTH, HEADS, HD)
        queries = rms_scaled(queries).astype(jnp.bfloat16).reshape(LENGTH * HEADS, HD)
        key_value = jnp.dot(sequence, w_kv, preferred_element_type=jnp.float32)
        keys = rms_scaled(key_value[:, :HD]).astype(jnp.bfloat16)
        values = key_value[:, HD:].astype(jnp.bfloat16)
        scores = jnp.dot(queries, keys.T, preferred_element_type=jnp.float32) * score_scale
        weights = jnp.exp(scores).astype(jnp.bfloat16)
        weighted = jnp.dot(weights, values, preferred_element_type=jnp.float32)
        totals = lax.optimization_barrier(jnp.sum(weights.astype(jnp.float32), axis=1, keepdims=True))
        context = (weighted / totals).astype(jnp.bfloat16).reshape(LENGTH, HEADS * HD)
        return jnp.dot(context, w_out, preferred_element_type=jnp.float32).astype(jnp.bfloat16)
    attention_out = lax.map(attend, attn_in)
    mixed_in = floats + attention_out.astype(jnp.float32)
    moe_in = (rms_scaled(mixed_in) * moe_gain).astype(jnp.bfloat16)
    flat_in = moe_in.reshape(-1, D)
    logits = jnp.dot(flat_in, router, preferred_element_type=jnp.float32)
    flat_ids = expert_ids.reshape(-1, TOP)
    chosen = jnp.take_along_axis(logits, flat_ids, axis=1)
    first = jax.nn.sigmoid(chosen[:, 0] - chosen[:, 1])
    blocks = DOMAINS * N_CTX
    block_ids = expert_ids.reshape(blocks, TOK_DEV * TOP)
    onehot = (block_ids[:, :, None] == jnp.arange(EXPERTS)[None, None, :]).astype(jnp.int32)
    earlier = jnp.cumsum(onehot, axis=1) - onehot
    slot = lax.optimization_barrier(jnp.sum(earlier * onehot, axis=2))
    column = (jnp.arange(blocks)[:, None] * CAP + slot).reshape(-1)
    expert = block_ids.reshape(-1)
    pair_rows = jnp.repeat(flat_in, TOP, axis=0)
    buffers = jnp.zeros((EXPERTS, blocks * CAP, D), jnp.bfloat16).at[expert, column].set(pair_rows)
    group_width = EFF // N_CTX

    def run_expert(operands):
        rows_in, gate_w, up_w, down_w = operands
        gated = jnp.dot(rows_in, gate_w, preferred_element_type=jnp.float32)
        lifted = jnp.dot(rows_in, up_w, preferred_element_type=jnp.float32)
        hidden = (jax.nn.silu(gated) * lifted).astype(jnp.bfloat16)
        total = jnp.zeros((rows_in.shape[0], D), jnp.float32)
        for group in range(N_CTX):
            term = jnp.dot(hidden[:, group * group_width:(group + 1) * group_width], down_w[group * group_width:(group + 1) * group_width], preferred_element_type=jnp.float32)
            total = total + lax.optimization_barrier(term.astype(jnp.bfloat16)).astype(jnp.float32)
        return total.astype(jnp.bfloat16)
    outputs = lax.map(run_expert, (buffers, w_gate, w_up, w_down))
    picked = outputs[expert, column].reshape(-1, TOP, D).astype(jnp.float32)
    mix = first[:, None] * picked[:, 0] + (1.0 - first)[:, None] * picked[:, 1]
    expert_mix = mix.astype(jnp.bfloat16).reshape(DOMAINS, LENGTH, D)
    return (attention_out, expert_mix)
```

```python
import functools

import jax
import jax.numpy as jnp
from jax import lax
from jax.experimental import pallas as pl
from jax.experimental.pallas import tpu as pltpu
from jax.sharding import PartitionSpec as P

HD = 128
TOP = 2
EPSILON = 1e-06
F32 = jnp.float32
BF16 = jnp.bfloat16
VMEM = pl.BlockSpec(memory_space=pltpu.VMEM)
SMEM = pl.BlockSpec(memory_space=pltpu.SMEM)


def rms_scaled(values):
    return values * lax.rsqrt(jnp.mean(values * values, axis=-1, keepdims=True) + EPSILON)


def swap(value, axis, bits):
    size = lax.axis_size(axis)
    return lax.ppermute(value, axis, [(i, i ^ bits) for i in range(size)])


def call(kernel, outs, scratch, flops, args, specs=None):
    moved = sum(a.size * a.dtype.itemsize for a in args) + sum(
        o.size * o.dtype.itemsize for o in outs
    )
    return pl.pallas_call(
        kernel,
        out_shape=outs,
        in_specs=[SMEM] + [VMEM] * (len(args) - 1) if specs is None else specs,
        out_specs=[VMEM] * len(outs),
        scratch_shapes=scratch,
        cost_estimate=pl.CostEstimate(flops=flops, bytes_accessed=moved, transcendentals=0),
        compiler_params=pltpu.CompilerParams(vmem_limit_bytes=48 * 1024 * 1024),
    )(*args)


def shape(rows, columns, kind=BF16):
    return jax.ShapeDtypeStruct((rows, columns), kind)


def project_kernel(count, heads, place, *refs):
    rows, weights = refs[:4], refs[4 : 4 + count]
    q_ref, kv_ref, whole, attn = refs[4 + count :]
    me, core = place[0], place[1]
    depth = weights[0].shape[0]
    for k, piece in enumerate(weights):
        start = pl.multiple_of(jnp.bitwise_xor(me, k) * depth, depth)
        whole[pl.ds(start, depth), :] = piece[...]
    block = rows[0].shape[0]
    for j, piece in enumerate(rows):
        spot = (j // 2) * 2 + jnp.bitwise_xor(core, j % 2)
        attn[pl.ds(pl.multiple_of(spot * block, block), block), :] = piece[...]
    for j in range(4):
        at = pl.ds(j * block, block)
        made = jnp.dot(attn[at, :], whole[...], preferred_element_type=F32)
        for h in range(heads):
            columns = slice(h * HD, (h + 1) * HD)
            q_ref[at, columns] = rms_scaled(made[:, columns]).astype(BF16)
        last = made[:, heads * HD :]
        scale = lax.rsqrt(jnp.mean(last * last, axis=-1, keepdims=True) + EPSILON)
        kv_ref[at, :] = (last * jnp.where(core == 0, scale, 1.0)).astype(BF16)


def attend_kernel(heads, place, q_ref, mine_ref, other_ref, near_ref, far_ref):
    core = place[1]
    mine, other = mine_ref[...], other_ref[...]
    keys = jnp.where(core == 0, mine, other)
    values = jnp.where(core == 0, other, mine)
    half = near_ref.shape[0]
    for out, base in ((far_ref, half), (near_ref, 0)):
        for h in range(heads):
            columns = slice(h * HD, (h + 1) * HD)
            scores = lax.dot_general(
                q_ref[base : base + half, columns],
                keys,
                (((1,), (1,)), ((), ())),
                preferred_element_type=F32,
            ) * (HD**-0.5)
            weights = jnp.exp(scores).astype(BF16)
            weighted = jnp.dot(weights, values, preferred_element_type=F32)
            totals = jnp.sum(weights.astype(F32), axis=1, keepdims=True)
            out[:, columns] = (weighted / totals).astype(BF16)


def route_kernel(count, capacity, blocks, place, *refs):
    contexts, own, theirs = refs[:4], refs[4 : 4 + count], refs[4 + count : 4 + 2 * count]
    tokens, gain, router, ids = refs[4 + 2 * count : 8 + 2 * count]
    outs = refs[8 + 2 * count :]
    attention_out, route, buffers = outs[0], outs[1], outs[2 : 2 + blocks]
    whole, context, total = outs[2 + blocks :]
    me, core, ctx = place[0], place[1], place[2]
    depth, half = own[0].shape
    wide = contexts[0].shape[1]
    for k in range(count):
        at = pl.ds(pl.multiple_of(jnp.bitwise_xor(me, k) * depth, depth), depth)
        whole[0, at, :] = own[k][...]
        whole[1, at, :] = theirs[k][...]
    for j, piece in enumerate(contexts):
        start = pl.multiple_of(jnp.bitwise_xor(ctx, j) * wide, wide)
        context[:, pl.ds(start, wide)] = piece[...]
    for j in range(2):
        start = pl.multiple_of(jnp.bitwise_xor(core, j) * half, half)
        total[:, pl.ds(start, half)] = jnp.dot(
            context[...], whole[j], preferred_element_type=F32
        )
    out = total[...].astype(BF16)
    attention_out[...] = out
    mixed = tokens[...].astype(F32) + out.astype(F32)
    moe_in = (rms_scaled(mixed) * gain[...]).astype(BF16)
    logits = jnp.dot(moe_in, router[...], preferred_element_type=F32)
    rows, experts = logits.shape
    lane = lax.broadcasted_iota(jnp.int32, (rows, experts), 1)
    first, second = ids[:, 0:1], ids[:, 1:2]
    is_first, is_second = lane == first, lane == second
    chosen = [
        jnp.sum(jnp.where(m, logits, 0.0), axis=1, keepdims=True) for m in (is_first, is_second)
    ]
    named = (is_first | is_second).astype(F32).astype(BF16)
    before = lax.broadcasted_iota(jnp.int32, (rows, rows), 0) > lax.broadcasted_iota(
        jnp.int32, (rows, rows), 1
    )
    earlier = jnp.dot(
        before.astype(F32).astype(BF16), named, preferred_element_type=F32
    )
    slots = [
        jnp.sum(jnp.where(m, earlier, 0.0), axis=1, keepdims=True).astype(jnp.int32)
        for m in (is_first, is_second)
    ]
    spots = [
        jnp.bitwise_xor(e, me) * capacity + s for e, s in zip((first, second), slots)
    ]
    gate = 1.0 / (1.0 + jnp.exp(chosen[1] - chosen[0]))
    column = lax.broadcasted_iota(jnp.int32, route.shape, 1)
    route[...] = jnp.where(
        column == 0,
        spots[0].astype(F32),
        jnp.where(column == 1, spots[1].astype(F32), gate),
    )
    lines = sum(b.shape[0] for b in buffers)
    place_of = lax.broadcasted_iota(jnp.int32, (rows, lines), 1)
    pick = ((place_of == spots[0]) | (place_of == spots[1])).astype(F32).astype(BF16)
    routed = lax.dot_general(
        pick, moe_in, (((0,), (0,)), ((), ())), preferred_element_type=F32
    ).astype(BF16)
    start = 0
    for b in buffers:
        b[...] = routed[start : start + b.shape[0]]
        start += b.shape[0]


def expert_kernel(parts, *refs):
    rows, (w_gate, w_up, w_down) = refs[:parts], refs[parts : parts + 3]
    outs, (joined, hidden) = refs[parts + 3 : 2 * parts + 3], refs[2 * parts + 3 :]
    start = 0
    for piece in rows:
        joined[start : start + piece.shape[0], :] = piece[...]
        start += piece.shape[0]
    width = 256
    for at in range(0, hidden.shape[1], width):
        columns = slice(at, at + width)
        gated = jnp.dot(joined[...], w_gate[:, columns], preferred_element_type=F32)
        lifted = jnp.dot(joined[...], w_up[:, columns], preferred_element_type=F32)
        hidden[:, columns] = (gated / (1.0 + jnp.exp(-gated)) * lifted).astype(BF16)
    for at in range(0, w_down.shape[1], width):
        columns = slice(at, at + width)
        made = jnp.dot(
            hidden[...], w_down[:, columns], preferred_element_type=F32
        ).astype(BF16)
        start = 0
        for out in outs:
            out[:, columns] = made[start : start + out.shape[0]]
            start += out.shape[0]


def add_kernel(pairs, *refs):
    lefts, rights, outs = refs[:pairs], refs[pairs : 2 * pairs], refs[2 * pairs :]
    share = len(outs) // pairs
    for i in range(pairs):
        start = 0
        for out in outs[i * share : (i + 1) * share]:
            at = slice(start, start + out.shape[0])
            out[...] = (lefts[i][at, :].astype(F32) + rights[i][at, :].astype(F32)).astype(BF16)
            start += out.shape[0]


def combine_kernel(count, *refs):
    route, blocks, out, joined = refs[0], refs[1 : 1 + count], refs[1 + count], refs[2 + count]
    start = 0
    for piece in blocks:
        joined[start : start + piece.shape[0], :] = piece[...]
        start += piece.shape[0]
    rows, lines = out.shape[0], joined.shape[0]
    place_of = lax.broadcasted_iota(jnp.int32, (rows, lines), 1).astype(F32)
    picked = [
        jnp.dot(
            (place_of == route[:, i : i + 1]).astype(F32).astype(BF16),
            joined[...],
            preferred_element_type=F32,
        )
        for i in range(2)
    ]
    gate = route[:, 2:3]
    out[...] = (gate * picked[0] + (1.0 - gate) * picked[1]).astype(BF16)


def add(lefts, rights, cuts):
    features = lefts[0].shape[1]
    outs = []
    for left in lefts:
        outs += [shape(left.shape[0] // cuts, features)] * cuts
    return call(
        functools.partial(add_kernel, len(lefts)),
        outs,
        [],
        sum(a.size for a in lefts),
        [*lefts, *rights],
        [VMEM] * (2 * len(lefts)),
    )


def gather(piece, small):
    if not small:
        return [lax.all_gather(piece, "exp", axis=0, tiled=True)]
    got = {0: piece}
    for bits in (6, 4, 2):
        got[bits] = swap(piece, "exp", bits)
    for bits in (0, 2, 4, 6):
        got[bits + 1] = swap(got[bits], "exp", 1)
    return [got[k] for k in range(8)]


def body(
    tokens, expert_ids, attn_gain, w_query, w_kv, w_out, moe_gain, router, w_gate, w_up, w_down
):
    features = tokens.shape[-1]
    inputs = tokens.reshape(-1, features)
    rows = inputs.shape[0]
    devices = lax.axis_size("exp")
    small = devices == 8
    ctx, position = lax.axis_index("ctx"), lax.axis_index("exp")
    core = ctx % 2
    me = position if small else jnp.zeros_like(position)
    place = jnp.stack([me, core, ctx]).astype(jnp.int32)
    heads = w_query.shape[1] // HD // lax.axis_size("ctx")

    attn_in = (rms_scaled(inputs.astype(F32)) * attn_gain).astype(BF16)
    piece = jnp.concatenate(
        [
            lax.dynamic_slice_in_dim(w_query, ctx * heads * HD, heads * HD, 1),
            lax.dynamic_slice_in_dim(w_kv, core * HD, HD, 1),
        ],
        axis=1,
    )
    weights = gather(piece, small)
    near = swap(attn_in, "ctx", 1)
    far = swap(attn_in, "ctx", 2)
    across = swap(far, "ctx", 1)
    half = w_out.shape[1] // 2
    out_piece = lax.dynamic_slice_in_dim(w_out, core * half, half, 1)
    out_own = gather(out_piece, small)
    out_theirs = [swap(w, "ctx", 1) for w in out_own]
    width = piece.shape[1]
    queries, mine = call(
        functools.partial(project_kernel, len(weights), heads),
        [shape(4 * rows, heads * HD), shape(4 * rows, HD)],
        [pltpu.VMEM((features, width), BF16), pltpu.VMEM((4 * rows, features), BF16)],
        8 * rows * features * width,
        [place, attn_in, near, far, across, *weights],
    )
    other = swap(mine, "ctx", 1)
    here, there = call(
        functools.partial(attend_kernel, heads),
        [shape(2 * rows, heads * HD)] * 2,
        [],
        16 * rows * rows * 4 * heads * HD,
        [place, queries, mine, other],
    )
    back = swap(there, "ctx", 2)

    def split(value):
        keep = lax.dynamic_slice_in_dim(value, core * rows, rows, 0)
        give = lax.dynamic_slice_in_dim(value, (1 - core) * rows, rows, 0)
        return keep, swap(give, "ctx", 1)

    context_0, context_1 = split(here)
    context_2, context_3 = split(back)

    experts = router.shape[1]
    capacity = max(2, 3 * rows * TOP // (2 * experts))
    lines = capacity * experts
    blocks = 8 if small else 1
    results = call(
        functools.partial(route_kernel, len(out_own), capacity, blocks),
        [shape(rows, features), shape(rows, 128, F32)]
        + [shape(lines // blocks, features)] * blocks,
        [
            pltpu.VMEM((2, w_out.shape[1], half), BF16),
            pltpu.VMEM((rows, w_out.shape[1]), BF16),
            pltpu.VMEM((rows, features), F32),
        ],
        2 * rows * features * (features + lines),
        [
            place,
            context_0,
            context_1,
            context_2,
            context_3,
            *out_own,
            *out_theirs,
            inputs,
            moe_gain.reshape(1, features),
            router,
            expert_ids.reshape(rows, TOP),
        ],
    )
    attention_out, route, buffers = results[0], results[1], results[2:]

    groups = ((0, 1, 2, 3), (4, 6), (5, 7)) if small else ((0,),)
    received = {}
    if small:
        received[0] = buffers[0]
        for k in (6, 4, 7, 5, 2, 3, 1):
            received[k] = swap(buffers[k], "exp", k)
    else:
        received[0] = lax.all_to_all(
            buffers[0], "exp", split_axis=0, concat_axis=0, tiled=True
        )
    returned = {}
    for group in groups:
        own = jnp.concatenate([received[k] for k in group]) if len(group) > 1 else received[group[0]]
        from_x = swap(own, "ctx", 2)
        from_core = swap(own, "ctx", 1)
        from_both = swap(from_x, "ctx", 1)
        taken = [own, from_x, from_core, from_both]
        count = own.shape[0]
        terms = call(
            functools.partial(expert_kernel, 4),
            [shape(count, features)] * 4,
            [
                pltpu.VMEM((4 * count, features), BF16),
                pltpu.VMEM((4 * count, w_gate.shape[-1]), BF16),
            ],
            24 * count * features * w_gate.shape[-1],
            [*taken, w_gate[0], w_up[0], w_down[0]],
            [VMEM] * 7,
        )
        core_x = swap(terms[3], "ctx", 1)
        core_own = swap(terms[2], "ctx", 1)
        (sum_x,) = add([terms[1]], [core_x], 1)
        x_own = swap(sum_x, "ctx", 2)
        (sum_own,) = add([terms[0]], [core_own], 1)
        for k, value in zip(group, add([sum_own], [x_own], len(group))):
            if small:
                returned[k] = swap(value, "exp", k) if k else value
            else:
                returned[k] = lax.all_to_all(
                    value, "exp", split_axis=0, concat_axis=0, tiled=True
                )
    (expert_mix,) = call(
        functools.partial(combine_kernel, blocks),
        [shape(rows, features)],
        [pltpu.VMEM((lines, features), BF16)],
        4 * rows * features * lines,
        [route, *[returned[k] for k in range(blocks)]],
        [VMEM] * (1 + blocks),
    )
    return (attention_out.reshape(tokens.shape), expert_mix.reshape(tokens.shape))


def solution(mesh):
    in_specs = (
        P("exp", "ctx", None),
        P("exp", "ctx", None),
        P(),
        P("exp", None),
        P("exp", None),
        P("exp", None),
        P(),
        P(),
        P("exp", None, "ctx"),
        P("exp", None, "ctx"),
        P("exp", "ctx", None),
    )
    out_specs = (P("exp", "ctx", None), P("exp", "ctx", None))
    return jax.shard_map(body, mesh=mesh, in_specs=in_specs, out_specs=out_specs, check_vma=False)
```

```python
import functools

import jax
import jax.numpy as jnp
from jax import lax
from jax.experimental import pallas as pl
from jax.experimental.pallas import tpu as pltpu
from jax.sharding import PartitionSpec as P

HD = 128
TOP = 2
EPSILON = 1e-06
F32 = jnp.float32
BF16 = jnp.bfloat16
VMEM = pl.BlockSpec(memory_space=pltpu.VMEM)
SMEM = pl.BlockSpec(memory_space=pltpu.SMEM)


def rms_scaled(values):
    return values * lax.rsqrt(jnp.mean(values * values, axis=-1, keepdims=True) + EPSILON)


def swap(value, axis, bits):
    size = lax.axis_size(axis)
    return lax.ppermute(value, axis, [(i, i ^ bits) for i in range(size)])


def call(kernel, outs, scratch, flops, args, specs=None):
    moved = sum(a.size * a.dtype.itemsize for a in args) + sum(
        o.size * o.dtype.itemsize for o in outs
    )
    return pl.pallas_call(
        kernel,
        out_shape=outs,
        in_specs=[SMEM] + [VMEM] * (len(args) - 1) if specs is None else specs,
        out_specs=[VMEM] * len(outs),
        scratch_shapes=scratch,
        cost_estimate=pl.CostEstimate(flops=flops * 1, bytes_accessed=moved * 1, transcendentals=0),
        compiler_params=pltpu.CompilerParams(vmem_limit_bytes=48 * 1024 * 1024),
    )(*args)


def shape(rows, columns, kind=BF16):
    return jax.ShapeDtypeStruct((rows, columns), kind)


def project_kernel(count, heads, place, *refs):
    rows, weights = refs[:4], refs[4 : 4 + count]
    q_ref, kv_ref, whole, attn = refs[4 + count :]
    me, core = place[0], place[1]
    depth = weights[0].shape[0]
    for k, piece in enumerate(weights):
        start = pl.multiple_of(jnp.bitwise_xor(me, k) * depth, depth)
        whole[pl.ds(start, depth), :] = piece[...]
    block = rows[0].shape[0]
    for j, piece in enumerate(rows):
        spot = (j // 2) * 2 + jnp.bitwise_xor(core, j % 2)
        attn[pl.ds(pl.multiple_of(spot * block, block), block), :] = piece[...]
    for j in range(4):
        at = pl.ds(j * block, block)
        made = jnp.dot(attn[at, :], whole[...], preferred_element_type=F32)
        for h in range(heads):
            columns = slice(h * HD, (h + 1) * HD)
            q_ref[at, columns] = rms_scaled(made[:, columns]).astype(BF16)
        last = made[:, heads * HD :]
        scale = lax.rsqrt(jnp.mean(last * last, axis=-1, keepdims=True) + EPSILON)
        kv_ref[at, :] = (last * jnp.where(core == 0, scale, 1.0)).astype(BF16)


def attend_kernel(heads, place, q_ref, mine_ref, other_ref, near_ref, far_ref):
    core = place[1]
    mine, other = mine_ref[...], other_ref[...]
    keys = jnp.where(core == 0, mine, other)
    values = jnp.where(core == 0, other, mine)
    half = near_ref.shape[0]
    for out, base in ((far_ref, half), (near_ref, 0)):
        for h in range(heads):
            columns = slice(h * HD, (h + 1) * HD)
            scores = lax.dot_general(
                q_ref[base : base + half, columns],
                keys,
                (((1,), (1,)), ((), ())),
                preferred_element_type=F32,
            ) * (HD**-0.5)
            weights = jnp.exp(scores).astype(BF16)
            weighted = jnp.dot(weights, values, preferred_element_type=F32)
            totals = jnp.sum(weights.astype(F32), axis=1, keepdims=True)
            out[:, columns] = (weighted / totals).astype(BF16)


def route_kernel(count, capacity, blocks, place, *refs):
    contexts, own, theirs = refs[:4], refs[4 : 4 + count], refs[4 + count : 4 + 2 * count]
    tokens, gain, router, ids = refs[4 + 2 * count : 8 + 2 * count]
    outs = refs[8 + 2 * count :]
    attention_out, route, buffers = outs[0], outs[1], outs[2 : 2 + blocks]
    whole, context, total = outs[2 + blocks :]
    me, core, ctx = place[0], place[1], place[2]
    depth, half = own[0].shape
    wide = contexts[0].shape[1]
    for k in range(count):
        at = pl.ds(pl.multiple_of(jnp.bitwise_xor(me, k) * depth, depth), depth)
        whole[0, at, :] = own[k][...]
        whole[1, at, :] = theirs[k][...]
    for j, piece in enumerate(contexts):
        start = pl.multiple_of(jnp.bitwise_xor(ctx, j) * wide, wide)
        context[:, pl.ds(start, wide)] = piece[...]
    for j in range(2):
        start = pl.multiple_of(jnp.bitwise_xor(core, j) * half, half)
        total[:, pl.ds(start, half)] = jnp.dot(
            context[...], whole[j], preferred_element_type=F32
        )
    out = total[...].astype(BF16)
    attention_out[...] = out
    mixed = tokens[...].astype(F32) + out.astype(F32)
    moe_in = (rms_scaled(mixed) * gain[...]).astype(BF16)
    logits = jnp.dot(moe_in, router[...], preferred_element_type=F32)
    rows, experts = logits.shape
    lane = lax.broadcasted_iota(jnp.int32, (rows, experts), 1)
    first, second = ids[:, 0:1], ids[:, 1:2]
    is_first, is_second = lane == first, lane == second
    chosen = [
        jnp.sum(jnp.where(m, logits, 0.0), axis=1, keepdims=True) for m in (is_first, is_second)
    ]
    named = (is_first | is_second).astype(F32).astype(BF16)
    before = lax.broadcasted_iota(jnp.int32, (rows, rows), 0) > lax.broadcasted_iota(
        jnp.int32, (rows, rows), 1
    )
    earlier = jnp.dot(
        before.astype(F32).astype(BF16), named, preferred_element_type=F32
    )
    slots = [
        jnp.sum(jnp.where(m, earlier, 0.0), axis=1, keepdims=True).astype(jnp.int32)
        for m in (is_first, is_second)
    ]
    spots = [
        jnp.bitwise_xor(e, me) * capacity + s for e, s in zip((first, second), slots)
    ]
    gate = 1.0 / (1.0 + jnp.exp(chosen[1] - chosen[0]))
    column = lax.broadcasted_iota(jnp.int32, route.shape, 1)
    route[...] = jnp.where(
        column == 0,
        spots[0].astype(F32),
        jnp.where(column == 1, spots[1].astype(F32), gate),
    )
    lines = sum(b.shape[0] for b in buffers)
    place_of = lax.broadcasted_iota(jnp.int32, (rows, lines), 1)
    pick = ((place_of == spots[0]) | (place_of == spots[1])).astype(F32).astype(BF16)
    routed = lax.dot_general(
        pick, moe_in, (((0,), (0,)), ((), ())), preferred_element_type=F32
    ).astype(BF16)
    start = 0
    for b in buffers:
        b[...] = routed[start : start + b.shape[0]]
        start += b.shape[0]


def expert_kernel(parts, *refs):
    rows, (w_gate, w_up, w_down) = refs[:parts], refs[parts : parts + 3]
    outs, (joined, hidden) = refs[parts + 3 : 2 * parts + 3], refs[2 * parts + 3 :]
    start = 0
    for piece in rows:
        joined[start : start + piece.shape[0], :] = piece[...]
        start += piece.shape[0]
    width = 256
    for at in range(0, hidden.shape[1], width):
        columns = slice(at, at + width)
        gated = jnp.dot(joined[...], w_gate[:, columns], preferred_element_type=F32)
        lifted = jnp.dot(joined[...], w_up[:, columns], preferred_element_type=F32)
        hidden[:, columns] = (gated / (1.0 + jnp.exp(-gated)) * lifted).astype(BF16)
    for at in range(0, w_down.shape[1], width):
        columns = slice(at, at + width)
        made = jnp.dot(
            hidden[...], w_down[:, columns], preferred_element_type=F32
        ).astype(BF16)
        start = 0
        for out in outs:
            out[:, columns] = made[start : start + out.shape[0]]
            start += out.shape[0]


def add_kernel(pairs, *refs):
    lefts, rights, outs = refs[:pairs], refs[pairs : 2 * pairs], refs[2 * pairs :]
    share = len(outs) // pairs
    for i in range(pairs):
        start = 0
        for out in outs[i * share : (i + 1) * share]:
            at = slice(start, start + out.shape[0])
            out[...] = (lefts[i][at, :].astype(F32) + rights[i][at, :].astype(F32)).astype(BF16)
            start += out.shape[0]


def combine_kernel(count, *refs):
    route, blocks, out, joined = refs[0], refs[1 : 1 + count], refs[1 + count], refs[2 + count]
    start = 0
    for piece in blocks:
        joined[start : start + piece.shape[0], :] = piece[...]
        start += piece.shape[0]
    rows, lines = out.shape[0], joined.shape[0]
    place_of = lax.broadcasted_iota(jnp.int32, (rows, lines), 1).astype(F32)
    picked = [
        jnp.dot(
            (place_of == route[:, i : i + 1]).astype(F32).astype(BF16),
            joined[...],
            preferred_element_type=F32,
        )
        for i in range(2)
    ]
    gate = route[:, 2:3]
    out[...] = (gate * picked[0] + (1.0 - gate) * picked[1]).astype(BF16)


def add(lefts, rights, cuts):
    features = lefts[0].shape[1]
    outs = []
    for left in lefts:
        outs += [shape(left.shape[0] // cuts, features)] * cuts
    return call(
        functools.partial(add_kernel, len(lefts)),
        outs,
        [],
        sum(a.size for a in lefts),
        [*lefts, *rights],
        [VMEM] * (2 * len(lefts)),
    )


def after(value, earlier):
    return lax.optimization_barrier((value, earlier))[0]


def gather(piece, small):
    if not small:
        return [lax.all_gather(piece, "exp", axis=0, tiled=True)]
    got = {0: piece}
    for bits in (6, 4, 2):
        got[bits] = swap(piece, "exp", bits)
    for bits in (0, 2, 4, 6):
        got[bits + 1] = swap(got[bits], "exp", 1)
    return [got[k] for k in range(8)]


def body(
    tokens, expert_ids, attn_gain, w_query, w_kv, w_out, moe_gain, router, w_gate, w_up, w_down
):
    features = tokens.shape[-1]
    inputs = tokens.reshape(-1, features)
    rows = inputs.shape[0]
    devices = lax.axis_size("exp")
    small = devices == 8
    ctx, position = lax.axis_index("ctx"), lax.axis_index("exp")
    core = ctx % 2
    me = position if small else jnp.zeros_like(position)
    place = jnp.stack([me, core, ctx]).astype(jnp.int32)
    heads = w_query.shape[1] // HD // lax.axis_size("ctx")

    attn_in = (rms_scaled(inputs.astype(F32)) * attn_gain).astype(BF16)
    piece = jnp.concatenate(
        [
            lax.dynamic_slice_in_dim(w_query, ctx * heads * HD, heads * HD, 1),
            lax.dynamic_slice_in_dim(w_kv, core * HD, HD, 1),
        ],
        axis=1,
    )
    weights = gather(piece, small)
    near = swap(attn_in, "ctx", 1)
    far = swap(attn_in, "ctx", 2)
    across = swap(far, "ctx", 1)
    half = w_out.shape[1] // 2
    out_piece = lax.dynamic_slice_in_dim(w_out, core * half, half, 1)
    out_own = gather(out_piece, small)
    out_theirs = [swap(w, "ctx", 1) for w in out_own]
    width = piece.shape[1]
    queries, mine = call(
        functools.partial(project_kernel, len(weights), heads),
        [shape(4 * rows, heads * HD), shape(4 * rows, HD)],
        [pltpu.VMEM((features, width), BF16), pltpu.VMEM((4 * rows, features), BF16)],
        8 * rows * features * width,
        [place, attn_in, near, far, across, *weights],
    )
    other = swap(mine, "ctx", 1)
    here, there = call(
        functools.partial(attend_kernel, heads),
        [shape(2 * rows, heads * HD)] * 2,
        [],
        16 * rows * rows * 4 * heads * HD,
        [place, queries, mine, other],
    )
    back = swap(there, "ctx", 2)

    def split(value):
        keep = lax.dynamic_slice_in_dim(value, core * rows, rows, 0)
        give = lax.dynamic_slice_in_dim(value, (1 - core) * rows, rows, 0)
        return keep, swap(give, "ctx", 1)

    context_0, context_1 = split(here)
    context_2, context_3 = split(back)

    experts = router.shape[1]
    capacity = max(2, 3 * rows * TOP // (2 * experts))
    lines = capacity * experts
    blocks = 8 if small else 1
    results = call(
        functools.partial(route_kernel, len(out_own), capacity, blocks),
        [shape(rows, features), shape(rows, 128, F32)]
        + [shape(lines // blocks, features)] * blocks,
        [
            pltpu.VMEM((2, w_out.shape[1], half), BF16),
            pltpu.VMEM((rows, w_out.shape[1]), BF16),
            pltpu.VMEM((rows, features), F32),
        ],
        2 * rows * features * (features + lines),
        [
            place,
            context_0,
            context_1,
            context_2,
            context_3,
            *out_own,
            *out_theirs,
            inputs,
            moe_gain.reshape(1, features),
            router,
            expert_ids.reshape(rows, TOP),
        ],
    )
    attention_out, route, buffers = results[0], results[1], results[2:]

    groups = ((4, 5), (6, 7), (0, 1, 2, 3)) if small else ((0,),)
    received = {}
    if small:
        received[0] = buffers[0]
        for k in (5, 4, 7, 6, 3, 2, 1):
            received[k] = swap(buffers[k], "exp", k)
    else:
        received[0] = lax.all_to_all(
            buffers[0], "exp", split_axis=0, concat_axis=0, tiled=True
        )
    owns, earlier = [], None
    for group in groups:
        blocks_in = [received[k] for k in group]
        if earlier is not None:
            blocks_in = [after(b, earlier) for b in blocks_in]
        own = jnp.concatenate(blocks_in) if len(group) > 1 else blocks_in[0]
        owns.append(own)
        earlier = own
    returned = {}
    earlier, waiting = None, None
    for group, own in zip(groups, owns):
        from_x = swap(own, "ctx", 2)
        from_core = swap(own, "ctx", 1)
        from_both = swap(from_x, "ctx", 1)
        taken = [own, from_x, from_core, from_both]
        if earlier is not None:
            taken = list(lax.optimization_barrier((*taken, *earlier))[:4])
        count = own.shape[0]
        terms = call(
            functools.partial(expert_kernel, 4),
            [shape(count, features)] * 4,
            [
                pltpu.VMEM((4 * count, features), BF16),
                pltpu.VMEM((4 * count, w_gate.shape[-1]), BF16),
            ],
            24 * count * features * w_gate.shape[-1],
            [*taken, w_gate[0], w_up[0], w_down[0]],
            [VMEM] * 7,
        )
        core_x = swap(terms[3], "ctx", 1)
        core_own = swap(terms[2], "ctx", 1)
        (sum_x,) = add([terms[1]], [core_x], 1)
        x_own = swap(sum_x, "ctx", 2)
        (sum_own,) = add([terms[0]], [core_own], 1)
        final = add([sum_own], [x_own], len(group))
        earlier = [sum_x, sum_own] + (waiting or [])
        waiting = list(final)
        for k, value in zip(group, final):
            if small:
                returned[k] = swap(value, "exp", k) if k else value
            else:
                returned[k] = lax.all_to_all(
                    value, "exp", split_axis=0, concat_axis=0, tiled=True
                )
    (expert_mix,) = call(
        functools.partial(combine_kernel, blocks),
        [shape(rows, features)],
        [pltpu.VMEM((lines, features), BF16)],
        4 * rows * features * lines,
        [route, *[returned[k] for k in range(blocks)]],
        [VMEM] * (1 + blocks),
    )
    return (attention_out.reshape(tokens.shape), expert_mix.reshape(tokens.shape))


def solution(mesh):
    in_specs = (
        P("exp", "ctx", None),
        P("exp", "ctx", None),
        P(),
        P("exp", None),
        P("exp", None),
        P("exp", None),
        P(),
        P(),
        P("exp", None, "ctx"),
        P("exp", None, "ctx"),
        P("exp", "ctx", None),
    )
    out_specs = (P("exp", "ctx", None), P("exp", "ctx", None))
    return jax.shard_map(body, mesh=mesh, in_specs=in_specs, out_specs=out_specs, check_vma=False)
```

```python
import functools

import jax
import jax.numpy as jnp
from jax import lax
from jax.experimental import pallas as pl
from jax.experimental.pallas import tpu as pltpu
from jax.sharding import PartitionSpec as P

HD = 128
TOP = 2
EPSILON = 1e-06
F32 = jnp.float32
BF16 = jnp.bfloat16
VMEM = pl.BlockSpec(memory_space=pltpu.VMEM)
SMEM = pl.BlockSpec(memory_space=pltpu.SMEM)


def rms_scaled(values):
    return values * lax.rsqrt(jnp.mean(values * values, axis=-1, keepdims=True) + EPSILON)


def swap(value, axis, bits):
    size = lax.axis_size(axis)
    return lax.ppermute(value, axis, [(i, i ^ bits) for i in range(size)])


def call(kernel, outs, scratch, flops, args, specs=None):
    moved = sum(a.size * a.dtype.itemsize for a in args) + sum(
        o.size * o.dtype.itemsize for o in outs
    )
    return pl.pallas_call(
        kernel,
        out_shape=outs,
        in_specs=[SMEM] + [VMEM] * (len(args) - 1) if specs is None else specs,
        out_specs=[VMEM] * len(outs),
        scratch_shapes=scratch,
        cost_estimate=pl.CostEstimate(flops=flops * 1, bytes_accessed=moved * 1, transcendentals=0),
        compiler_params=pltpu.CompilerParams(vmem_limit_bytes=48 * 1024 * 1024),
    )(*args)


def shape(rows, columns, kind=BF16):
    return jax.ShapeDtypeStruct((rows, columns), kind)


def project_kernel(count, heads, place, *refs):
    rows, weights = refs[:4], refs[4 : 4 + count]
    q_ref, kv_ref, whole, attn = refs[4 + count :]
    me, core = place[0], place[1]
    depth = weights[0].shape[0]
    for k, piece in enumerate(weights):
        start = pl.multiple_of(jnp.bitwise_xor(me, k) * depth, depth)
        whole[pl.ds(start, depth), :] = piece[...]
    block = rows[0].shape[0]
    for j, piece in enumerate(rows):
        spot = (j // 2) * 2 + jnp.bitwise_xor(core, j % 2)
        attn[pl.ds(pl.multiple_of(spot * block, block), block), :] = piece[...]
    for j in range(4):
        at = pl.ds(j * block, block)
        made = jnp.dot(attn[at, :], whole[...], preferred_element_type=F32)
        for h in range(heads):
            columns = slice(h * HD, (h + 1) * HD)
            q_ref[at, columns] = rms_scaled(made[:, columns]).astype(BF16)
        last = made[:, heads * HD :]
        scale = lax.rsqrt(jnp.mean(last * last, axis=-1, keepdims=True) + EPSILON)
        kv_ref[at, :] = (last * jnp.where(core == 0, scale, 1.0)).astype(BF16)


def attend_kernel(heads, place, q_ref, mine_ref, other_ref, near_ref, far_ref):
    core = place[1]
    mine, other = mine_ref[...], other_ref[...]
    keys = jnp.where(core == 0, mine, other)
    values = jnp.where(core == 0, other, mine)
    half = near_ref.shape[0]
    for out, base in ((far_ref, half), (near_ref, 0)):
        for h in range(heads):
            columns = slice(h * HD, (h + 1) * HD)
            scores = lax.dot_general(
                q_ref[base : base + half, columns],
                keys,
                (((1,), (1,)), ((), ())),
                preferred_element_type=F32,
            ) * (HD**-0.5)
            weights = jnp.exp(scores).astype(BF16)
            weighted = jnp.dot(weights, values, preferred_element_type=F32)
            totals = jnp.sum(weights.astype(F32), axis=1, keepdims=True)
            out[:, columns] = (weighted / totals).astype(BF16)


def route_kernel(count, capacity, blocks, place, *refs):
    contexts, own, theirs = refs[:4], refs[4 : 4 + count], refs[4 + count : 4 + 2 * count]
    tokens, gain, router, ids = refs[4 + 2 * count : 8 + 2 * count]
    outs = refs[8 + 2 * count :]
    attention_out, route, buffers = outs[0], outs[1], outs[2 : 2 + blocks]
    whole, context, total = outs[2 + blocks :]
    me, core, ctx = place[0], place[1], place[2]
    depth, half = own[0].shape
    wide = contexts[0].shape[1]
    for k in range(count):
        at = pl.ds(pl.multiple_of(jnp.bitwise_xor(me, k) * depth, depth), depth)
        whole[0, at, :] = own[k][...]
        whole[1, at, :] = theirs[k][...]
    for j, piece in enumerate(contexts):
        start = pl.multiple_of(jnp.bitwise_xor(ctx, j) * wide, wide)
        context[:, pl.ds(start, wide)] = piece[...]
    for j in range(2):
        start = pl.multiple_of(jnp.bitwise_xor(core, j) * half, half)
        total[:, pl.ds(start, half)] = jnp.dot(
            context[...], whole[j], preferred_element_type=F32
        )
    out = total[...].astype(BF16)
    attention_out[...] = out
    mixed = tokens[...].astype(F32) + out.astype(F32)
    moe_in = (rms_scaled(mixed) * gain[...]).astype(BF16)
    logits = jnp.dot(moe_in, router[...], preferred_element_type=F32)
    rows, experts = logits.shape
    lane = lax.broadcasted_iota(jnp.int32, (rows, experts), 1)
    first, second = ids[:, 0:1], ids[:, 1:2]
    is_first, is_second = lane == first, lane == second
    chosen = [
        jnp.sum(jnp.where(m, logits, 0.0), axis=1, keepdims=True) for m in (is_first, is_second)
    ]
    named = (is_first | is_second).astype(F32).astype(BF16)
    before = lax.broadcasted_iota(jnp.int32, (rows, rows), 0) > lax.broadcasted_iota(
        jnp.int32, (rows, rows), 1
    )
    earlier = jnp.dot(
        before.astype(F32).astype(BF16), named, preferred_element_type=F32
    )
    slots = [
        jnp.sum(jnp.where(m, earlier, 0.0), axis=1, keepdims=True).astype(jnp.int32)
        for m in (is_first, is_second)
    ]
    spots = [
        jnp.bitwise_xor(e, me) * capacity + s for e, s in zip((first, second), slots)
    ]
    gate = 1.0 / (1.0 + jnp.exp(chosen[1] - chosen[0]))
    column = lax.broadcasted_iota(jnp.int32, route.shape, 1)
    route[...] = jnp.where(
        column == 0,
        spots[0].astype(F32),
        jnp.where(column == 1, spots[1].astype(F32), gate),
    )
    lines = sum(b.shape[0] for b in buffers)
    place_of = lax.broadcasted_iota(jnp.int32, (rows, lines), 1)
    pick = ((place_of == spots[0]) | (place_of == spots[1])).astype(F32).astype(BF16)
    routed = lax.dot_general(
        pick, moe_in, (((0,), (0,)), ((), ())), preferred_element_type=F32
    ).astype(BF16)
    start = 0
    for b in buffers:
        b[...] = routed[start : start + b.shape[0]]
        start += b.shape[0]


def expert_kernel(parts, *refs):
    rows, (w_gate, w_up, w_down) = refs[:parts], refs[parts : parts + 3]
    outs, (joined, hidden) = refs[parts + 3 : 2 * parts + 3], refs[2 * parts + 3 :]
    start = 0
    for piece in rows:
        joined[start : start + piece.shape[0], :] = piece[...]
        start += piece.shape[0]
    width = 256
    for at in range(0, hidden.shape[1], width):
        columns = slice(at, at + width)
        gated = jnp.dot(joined[...], w_gate[:, columns], preferred_element_type=F32)
        lifted = jnp.dot(joined[...], w_up[:, columns], preferred_element_type=F32)
        hidden[:, columns] = (gated / (1.0 + jnp.exp(-gated)) * lifted).astype(BF16)
    for at in range(0, w_down.shape[1], width):
        columns = slice(at, at + width)
        made = jnp.dot(
            hidden[...], w_down[:, columns], preferred_element_type=F32
        ).astype(BF16)
        start = 0
        for out in outs:
            out[:, columns] = made[start : start + out.shape[0]]
            start += out.shape[0]


def add_kernel(pairs, *refs):
    lefts, rights, outs = refs[:pairs], refs[pairs : 2 * pairs], refs[2 * pairs :]
    share = len(outs) // pairs
    for i in range(pairs):
        start = 0
        for out in outs[i * share : (i + 1) * share]:
            at = slice(start, start + out.shape[0])
            out[...] = (lefts[i][at, :].astype(F32) + rights[i][at, :].astype(F32)).astype(BF16)
            start += out.shape[0]


def combine_kernel(count, *refs):
    route, blocks, out, joined = refs[0], refs[1 : 1 + count], refs[1 + count], refs[2 + count]
    start = 0
    for piece in blocks:
        joined[start : start + piece.shape[0], :] = piece[...]
        start += piece.shape[0]
    rows, lines = out.shape[0], joined.shape[0]
    place_of = lax.broadcasted_iota(jnp.int32, (rows, lines), 1).astype(F32)
    picked = [
        jnp.dot(
            (place_of == route[:, i : i + 1]).astype(F32).astype(BF16),
            joined[...],
            preferred_element_type=F32,
        )
        for i in range(2)
    ]
    gate = route[:, 2:3]
    out[...] = (gate * picked[0] + (1.0 - gate) * picked[1]).astype(BF16)


def add(lefts, rights, cuts):
    features = lefts[0].shape[1]
    outs = []
    for left in lefts:
        outs += [shape(left.shape[0] // cuts, features)] * cuts
    return call(
        functools.partial(add_kernel, len(lefts)),
        outs,
        [],
        sum(a.size for a in lefts),
        [*lefts, *rights],
        [VMEM] * (2 * len(lefts)),
    )


def after(value, earlier):
    return lax.optimization_barrier((value, earlier))[0]


def gather(piece, small):
    if not small:
        return [lax.all_gather(piece, "exp", axis=0, tiled=True)]
    got = {0: piece}
    for bits in (6, 4, 2):
        got[bits] = swap(piece, "exp", bits)
    for bits in (0, 2, 4, 6):
        got[bits + 1] = swap(got[bits], "exp", 1)
    return [got[k] for k in range(8)]


def body(
    tokens, expert_ids, attn_gain, w_query, w_kv, w_out, moe_gain, router, w_gate, w_up, w_down
):
    features = tokens.shape[-1]
    inputs = tokens.reshape(-1, features)
    rows = inputs.shape[0]
    devices = lax.axis_size("exp")
    small = devices == 8
    ctx, position = lax.axis_index("ctx"), lax.axis_index("exp")
    core = ctx % 2
    me = position if small else jnp.zeros_like(position)
    place = jnp.stack([me, core, ctx]).astype(jnp.int32)
    heads = w_query.shape[1] // HD // lax.axis_size("ctx")

    piece = jnp.concatenate(
        [
            lax.dynamic_slice_in_dim(w_query, ctx * heads * HD, heads * HD, 1),
            lax.dynamic_slice_in_dim(w_kv, core * HD, HD, 1),
        ],
        axis=1,
    )
    weights = gather(piece, small)
    held = after(inputs, piece) if small else inputs
    attn_in = (rms_scaled(held.astype(F32)) * attn_gain).astype(BF16)
    near = swap(attn_in, "ctx", 1)
    far = swap(attn_in, "ctx", 2)
    across = swap(far, "ctx", 1)
    half = w_out.shape[1] // 2
    out_piece = lax.dynamic_slice_in_dim(w_out, core * half, half, 1)
    out_own = gather(out_piece, small)
    out_theirs = [swap(w, "ctx", 1) for w in out_own]
    width = piece.shape[1]
    queries, mine = call(
        functools.partial(project_kernel, len(weights), heads),
        [shape(4 * rows, heads * HD), shape(4 * rows, HD)],
        [pltpu.VMEM((features, width), BF16), pltpu.VMEM((4 * rows, features), BF16)],
        8 * rows * features * width,
        [place, attn_in, near, far, across, *weights],
    )
    other = swap(mine, "ctx", 1)
    here, there = call(
        functools.partial(attend_kernel, heads),
        [shape(2 * rows, heads * HD)] * 2,
        [],
        16 * rows * rows * 4 * heads * HD,
        [place, queries, mine, other],
    )
    back = swap(there, "ctx", 2)

    def split(value):
        keep = lax.dynamic_slice_in_dim(value, core * rows, rows, 0)
        give = lax.dynamic_slice_in_dim(value, (1 - core) * rows, rows, 0)
        return keep, swap(give, "ctx", 1)

    context_0, context_1 = split(here)
    context_2, context_3 = split(back)

    experts = router.shape[1]
    capacity = max(2, 3 * rows * TOP // (2 * experts))
    lines = capacity * experts
    blocks = 8 if small else 1
    results = call(
        functools.partial(route_kernel, len(out_own), capacity, blocks),
        [shape(rows, features), shape(rows, 128, F32)]
        + [shape(lines // blocks, features)] * blocks,
        [
            pltpu.VMEM((2, w_out.shape[1], half), BF16),
            pltpu.VMEM((rows, w_out.shape[1]), BF16),
            pltpu.VMEM((rows, features), F32),
        ],
        2 * rows * features * (features + lines),
        [
            place,
            context_0,
            context_1,
            context_2,
            context_3,
            *out_own,
            *out_theirs,
            inputs,
            moe_gain.reshape(1, features),
            router,
            expert_ids.reshape(rows, TOP),
        ],
    )
    attention_out, route, buffers = results[0], results[1], results[2:]

    groups = ((4, 5), (6, 7), (0, 1, 2, 3)) if small else ((0,),)
    received = {}
    if small:
        received[0] = buffers[0]
        for k in (5, 4, 7, 6, 3, 2, 1):
            received[k] = swap(buffers[k], "exp", k)
    else:
        received[0] = lax.all_to_all(
            buffers[0], "exp", split_axis=0, concat_axis=0, tiled=True
        )
    owns, earlier = [], None
    for group in groups:
        blocks_in = [received[k] for k in group]
        if earlier is not None:
            blocks_in = [after(b, earlier) for b in blocks_in]
        own = jnp.concatenate(blocks_in) if len(group) > 1 else blocks_in[0]
        owns.append(own)
        earlier = own
    returned = {}
    earlier, waiting = None, None
    xs, rets = [], []
    for group, own in zip(groups, owns):
        from_x = swap(after(own, xs[-2]) if len(xs) > 1 else own, "ctx", 2)
        xs.append(from_x)
        from_core = swap(own, "ctx", 1)
        from_both = swap(from_x, "ctx", 1)
        taken = [own, from_x, from_core, from_both]
        if earlier is not None:
            taken = list(lax.optimization_barrier((*taken, *earlier))[:4])
        count = own.shape[0]
        terms = call(
            functools.partial(expert_kernel, 4),
            [shape(count, features)] * 4,
            [
                pltpu.VMEM((4 * count, features), BF16),
                pltpu.VMEM((4 * count, w_gate.shape[-1]), BF16),
            ],
            24 * count * features * w_gate.shape[-1],
            [*taken, w_gate[0], w_up[0], w_down[0]],
            [VMEM] * 7,
        )
        core_x = swap(terms[3], "ctx", 1)
        core_own = swap(terms[2], "ctx", 1)
        (sum_x,) = add([terms[1]], [core_x], 1)
        x_own = swap(after(sum_x, rets[-1]) if rets else sum_x, "ctx", 2)
        rets.append(x_own)
        (sum_own,) = add([terms[0]], [core_own], 1)
        final = add([sum_own], [x_own], len(group))
        earlier = [sum_x, sum_own] + (waiting or [])
        waiting = list(final)
        for k, value in zip(group, final):
            if small:
                returned[k] = swap(value, "exp", k) if k else value
            else:
                returned[k] = lax.all_to_all(
                    value, "exp", split_axis=0, concat_axis=0, tiled=True
                )
    (expert_mix,) = call(
        functools.partial(combine_kernel, blocks),
        [shape(rows, features)],
        [pltpu.VMEM((lines, features), BF16)],
        4 * rows * features * lines,
        [route, *[returned[k] for k in range(blocks)]],
        [VMEM] * (1 + blocks),
    )
    return (attention_out.reshape(tokens.shape), expert_mix.reshape(tokens.shape))


def solution(mesh):
    in_specs = (
        P("exp", "ctx", None),
        P("exp", "ctx", None),
        P(),
        P("exp", None),
        P("exp", None),
        P("exp", None),
        P(),
        P(),
        P("exp", None, "ctx"),
        P("exp", None, "ctx"),
        P("exp", "ctx", None),
    )
    out_specs = (P("exp", "ctx", None), P("exp", "ctx", None))
    return jax.shard_map(body, mesh=mesh, in_specs=in_specs, out_specs=out_specs, check_vma=False)
```

```python
import functools

import jax
import jax.numpy as jnp
from jax import lax
from jax.experimental import pallas as pl
from jax.experimental.pallas import tpu as pltpu
from jax.sharding import PartitionSpec as P

HD = 128
TOP = 2
EPSILON = 1e-06
F32 = jnp.float32
BF16 = jnp.bfloat16
VMEM = pl.BlockSpec(memory_space=pltpu.VMEM)
SMEM = pl.BlockSpec(memory_space=pltpu.SMEM)


def rms_scaled(values):
    return values * lax.rsqrt(jnp.mean(values * values, axis=-1, keepdims=True) + EPSILON)


def swap(value, axis, bits):
    size = lax.axis_size(axis)
    return lax.ppermute(value, axis, [(i, i ^ bits) for i in range(size)])


def call(kernel, outs, scratch, flops, args, specs=None):
    moved = sum(a.size * a.dtype.itemsize for a in args) + sum(
        o.size * o.dtype.itemsize for o in outs
    )
    return pl.pallas_call(
        kernel,
        out_shape=outs,
        in_specs=[SMEM] + [VMEM] * (len(args) - 1) if specs is None else specs,
        out_specs=[VMEM] * len(outs),
        scratch_shapes=scratch,
        cost_estimate=pl.CostEstimate(flops=flops * 1, bytes_accessed=moved * 1, transcendentals=0),
        compiler_params=pltpu.CompilerParams(vmem_limit_bytes=48 * 1024 * 1024),
    )(*args)


def shape(rows, columns, kind=BF16):
    return jax.ShapeDtypeStruct((rows, columns), kind)


def project_kernel(count, heads, place, *refs):
    rows, weights = refs[:4], refs[4 : 4 + count]
    q_ref, kv_ref, whole, attn = refs[4 + count :]
    me, core = place[0], place[1]
    depth = weights[0].shape[0]
    for k, piece in enumerate(weights):
        start = pl.multiple_of(jnp.bitwise_xor(me, k) * depth, depth)
        whole[pl.ds(start, depth), :] = piece[...]
    block = rows[0].shape[0]
    for j, piece in enumerate(rows):
        spot = (j // 2) * 2 + jnp.bitwise_xor(core, j % 2)
        attn[pl.ds(pl.multiple_of(spot * block, block), block), :] = piece[...]
    for j in range(4):
        at = pl.ds(j * block, block)
        made = jnp.dot(attn[at, :], whole[...], preferred_element_type=F32)
        for h in range(heads):
            columns = slice(h * HD, (h + 1) * HD)
            q_ref[at, columns] = rms_scaled(made[:, columns]).astype(BF16)
        last = made[:, heads * HD :]
        scale = lax.rsqrt(jnp.mean(last * last, axis=-1, keepdims=True) + EPSILON)
        kv_ref[at, :] = (last * jnp.where(core == 0, scale, 1.0)).astype(BF16)


def attend_kernel(heads, place, q_ref, mine_ref, other_ref, near_ref, far_ref):
    core = place[1]
    mine, other = mine_ref[...], other_ref[...]
    keys = jnp.where(core == 0, mine, other)
    values = jnp.where(core == 0, other, mine)
    half = near_ref.shape[0]
    for out, base in ((far_ref, half), (near_ref, 0)):
        for h in range(heads):
            columns = slice(h * HD, (h + 1) * HD)
            scores = lax.dot_general(
                q_ref[base : base + half, columns],
                keys,
                (((1,), (1,)), ((), ())),
                preferred_element_type=F32,
            ) * (HD**-0.5)
            weights = jnp.exp(scores).astype(BF16)
            weighted = jnp.dot(weights, values, preferred_element_type=F32)
            totals = jnp.sum(weights.astype(F32), axis=1, keepdims=True)
            out[:, columns] = (weighted / totals).astype(BF16)


def route_kernel(count, capacity, blocks, place, *refs):
    contexts, own, theirs = refs[:4], refs[4 : 4 + count], refs[4 + count : 4 + 2 * count]
    tokens, gain, router, ids = refs[4 + 2 * count : 8 + 2 * count]
    outs = refs[8 + 2 * count :]
    attention_out, route, buffers = outs[0], outs[1], outs[2 : 2 + blocks]
    whole, context, total = outs[2 + blocks :]
    me, core, ctx = place[0], place[1], place[2]
    depth, half = own[0].shape
    wide = contexts[0].shape[1]
    for k in range(count):
        at = pl.ds(pl.multiple_of(jnp.bitwise_xor(me, k) * depth, depth), depth)
        whole[0, at, :] = own[k][...]
        whole[1, at, :] = theirs[k][...]
    for j, piece in enumerate(contexts):
        start = pl.multiple_of(jnp.bitwise_xor(ctx, j) * wide, wide)
        context[:, pl.ds(start, wide)] = piece[...]
    for j in range(2):
        start = pl.multiple_of(jnp.bitwise_xor(core, j) * half, half)
        total[:, pl.ds(start, half)] = jnp.dot(
            context[...], whole[j], preferred_element_type=F32
        )
    out = total[...].astype(BF16)
    attention_out[...] = out
    mixed = tokens[...].astype(F32) + out.astype(F32)
    moe_in = (rms_scaled(mixed) * gain[...]).astype(BF16)
    logits = jnp.dot(moe_in, router[...], preferred_element_type=F32)
    rows, experts = logits.shape
    lane = lax.broadcasted_iota(jnp.int32, (rows, experts), 1)
    first, second = ids[:, 0:1], ids[:, 1:2]
    is_first, is_second = lane == first, lane == second
    chosen = [
        jnp.sum(jnp.where(m, logits, 0.0), axis=1, keepdims=True) for m in (is_first, is_second)
    ]
    named = (is_first | is_second).astype(F32).astype(BF16)
    before = lax.broadcasted_iota(jnp.int32, (rows, rows), 0) > lax.broadcasted_iota(
        jnp.int32, (rows, rows), 1
    )
    earlier = jnp.dot(
        before.astype(F32).astype(BF16), named, preferred_element_type=F32
    )
    slots = [
        jnp.sum(jnp.where(m, earlier, 0.0), axis=1, keepdims=True).astype(jnp.int32)
        for m in (is_first, is_second)
    ]
    spots = [
        jnp.bitwise_xor(e, me) * capacity + s for e, s in zip((first, second), slots)
    ]
    gate = 1.0 / (1.0 + jnp.exp(chosen[1] - chosen[0]))
    column = lax.broadcasted_iota(jnp.int32, route.shape, 1)
    route[...] = jnp.where(
        column == 0,
        spots[0].astype(F32),
        jnp.where(column == 1, spots[1].astype(F32), gate),
    )
    lines = sum(b.shape[0] for b in buffers)
    place_of = lax.broadcasted_iota(jnp.int32, (rows, lines), 1)
    pick = ((place_of == spots[0]) | (place_of == spots[1])).astype(F32).astype(BF16)
    routed = lax.dot_general(
        pick, moe_in, (((0,), (0,)), ((), ())), preferred_element_type=F32
    ).astype(BF16)
    start = 0
    for b in buffers:
        b[...] = routed[start : start + b.shape[0]]
        start += b.shape[0]


def expert_kernel(parts, *refs):
    rows, (w_gate, w_up, w_down) = refs[:parts], refs[parts : parts + 3]
    outs, (joined, hidden) = refs[parts + 3 : 2 * parts + 3], refs[2 * parts + 3 :]
    start = 0
    for piece in rows:
        joined[start : start + piece.shape[0], :] = piece[...]
        start += piece.shape[0]
    width = 256
    for at in range(0, hidden.shape[1], width):
        columns = slice(at, at + width)
        gated = jnp.dot(joined[...], w_gate[:, columns], preferred_element_type=F32)
        lifted = jnp.dot(joined[...], w_up[:, columns], preferred_element_type=F32)
        hidden[:, columns] = (gated / (1.0 + jnp.exp(-gated)) * lifted).astype(BF16)
    for at in range(0, w_down.shape[1], width):
        columns = slice(at, at + width)
        made = jnp.dot(
            hidden[...], w_down[:, columns], preferred_element_type=F32
        ).astype(BF16)
        start = 0
        for out in outs:
            out[:, columns] = made[start : start + out.shape[0]]
            start += out.shape[0]


def add_kernel(pairs, *refs):
    lefts, rights, outs = refs[:pairs], refs[pairs : 2 * pairs], refs[2 * pairs :]
    share = len(outs) // pairs
    for i in range(pairs):
        start = 0
        for out in outs[i * share : (i + 1) * share]:
            at = slice(start, start + out.shape[0])
            out[...] = (lefts[i][at, :].astype(F32) + rights[i][at, :].astype(F32)).astype(BF16)
            start += out.shape[0]


def combine_kernel(count, *refs):
    route, blocks, out, joined = refs[0], refs[1 : 1 + count], refs[1 + count], refs[2 + count]
    start = 0
    for piece in blocks:
        joined[start : start + piece.shape[0], :] = piece[...]
        start += piece.shape[0]
    rows, lines = out.shape[0], joined.shape[0]
    place_of = lax.broadcasted_iota(jnp.int32, (rows, lines), 1).astype(F32)
    picked = [
        jnp.dot(
            (place_of == route[:, i : i + 1]).astype(F32).astype(BF16),
            joined[...],
            preferred_element_type=F32,
        )
        for i in range(2)
    ]
    gate = route[:, 2:3]
    out[...] = (gate * picked[0] + (1.0 - gate) * picked[1]).astype(BF16)


def add(lefts, rights, cuts):
    features = lefts[0].shape[1]
    outs = []
    for left in lefts:
        outs += [shape(left.shape[0] // cuts, features)] * cuts
    return call(
        functools.partial(add_kernel, len(lefts)),
        outs,
        [],
        sum(a.size for a in lefts),
        [*lefts, *rights],
        [VMEM] * (2 * len(lefts)),
    )


def after(value, earlier):
    return lax.optimization_barrier((value, earlier))[0]


def gather(piece, small):
    if not small:
        return [lax.all_gather(piece, "exp", axis=0, tiled=True)]
    got = {0: piece}
    for bits in (6, 4, 2):
        got[bits] = swap(piece, "exp", bits)
    for bits in (0, 2, 4, 6):
        got[bits + 1] = swap(got[bits], "exp", 1)
    return [got[k] for k in range(8)]


def body(
    tokens, expert_ids, attn_gain, w_query, w_kv, w_out, moe_gain, router, w_gate, w_up, w_down
):
    features = tokens.shape[-1]
    inputs = tokens.reshape(-1, features)
    rows = inputs.shape[0]
    devices = lax.axis_size("exp")
    small = devices == 8
    ctx, position = lax.axis_index("ctx"), lax.axis_index("exp")
    core = ctx % 2
    me = position if small else jnp.zeros_like(position)
    place = jnp.stack([me, core, ctx]).astype(jnp.int32)
    heads = w_query.shape[1] // HD // lax.axis_size("ctx")

    piece = jnp.concatenate(
        [
            lax.dynamic_slice_in_dim(w_query, ctx * heads * HD, heads * HD, 1),
            lax.dynamic_slice_in_dim(w_kv, core * HD, HD, 1),
        ],
        axis=1,
    )
    weights = gather(piece, small)
    held = after(inputs, piece) if small else inputs
    attn_in = (rms_scaled(held.astype(F32)) * attn_gain).astype(BF16)
    near = swap(attn_in, "ctx", 1)
    far = swap(attn_in, "ctx", 2)
    across = swap(far, "ctx", 1)
    half = w_out.shape[1] // 2
    out_piece = lax.dynamic_slice_in_dim(w_out, core * half, half, 1)
    out_own = gather(out_piece, small)
    out_theirs = [swap(w, "ctx", 1) for w in out_own]
    width = piece.shape[1]
    queries, mine = call(
        functools.partial(project_kernel, len(weights), heads),
        [shape(4 * rows, heads * HD), shape(4 * rows, HD)],
        [pltpu.VMEM((features, width), BF16), pltpu.VMEM((4 * rows, features), BF16)],
        8 * rows * features * width,
        [place, attn_in, near, far, across, *weights],
    )
    other = swap(mine, "ctx", 1)
    here, there = call(
        functools.partial(attend_kernel, heads),
        [shape(2 * rows, heads * HD)] * 2,
        [],
        16 * rows * rows * 4 * heads * HD,
        [place, queries, mine, other],
    )
    back = swap(there, "ctx", 2)

    def split(value):
        keep = lax.dynamic_slice_in_dim(value, core * rows, rows, 0)
        give = lax.dynamic_slice_in_dim(value, (1 - core) * rows, rows, 0)
        return keep, swap(give, "ctx", 1)

    context_0, context_1 = split(here)
    context_2, context_3 = split(back)

    experts = router.shape[1]
    capacity = max(2, 3 * rows * TOP // (2 * experts))
    lines = capacity * experts
    blocks = 8 if small else 1
    results = call(
        functools.partial(route_kernel, len(out_own), capacity, blocks),
        [shape(rows, features), shape(rows, 128, F32)]
        + [shape(lines // blocks, features)] * blocks,
        [
            pltpu.VMEM((2, w_out.shape[1], half), BF16),
            pltpu.VMEM((rows, w_out.shape[1]), BF16),
            pltpu.VMEM((rows, features), F32),
        ],
        2 * rows * features * (features + lines),
        [
            place,
            context_0,
            context_1,
            context_2,
            context_3,
            *out_own,
            *out_theirs,
            inputs,
            moe_gain.reshape(1, features),
            router,
            expert_ids.reshape(rows, TOP),
        ],
    )
    attention_out, route, buffers = results[0], results[1], results[2:]

    groups = ((6, 7), (4, 5), (0, 1, 2, 3)) if small else ((0,),)
    received = {}
    if small:
        received[0] = buffers[0]
        for k in (5, 4, 7, 6, 3, 2, 1):
            received[k] = swap(buffers[k], "exp", k)
    else:
        received[0] = lax.all_to_all(
            buffers[0], "exp", split_axis=0, concat_axis=0, tiled=True
        )
    owns, earlier = [], None
    for group in groups:
        blocks_in = [received[k] for k in group]
        if earlier is not None:
            blocks_in = [after(b, earlier) for b in blocks_in]
        own = jnp.concatenate(blocks_in) if len(group) > 1 else blocks_in[0]
        owns.append(own)
        earlier = own
    returned = {}
    earlier, waiting = None, None
    xs, rets = [], []
    for group, own in zip(groups, owns):
        from_x = swap(after(own, xs[-2]) if len(xs) > 1 else own, "ctx", 2)
        xs.append(from_x)
        from_core = swap(own, "ctx", 1)
        from_both = swap(from_x, "ctx", 1)
        taken = [own, from_x, from_core, from_both]
        if earlier is not None:
            taken = list(lax.optimization_barrier((*taken, *earlier))[:4])
        count = own.shape[0]
        terms = call(
            functools.partial(expert_kernel, 4),
            [shape(count, features)] * 4,
            [
                pltpu.VMEM((4 * count, features), BF16),
                pltpu.VMEM((4 * count, w_gate.shape[-1]), BF16),
            ],
            24 * count * features * w_gate.shape[-1],
            [*taken, w_gate[0], w_up[0], w_down[0]],
            [VMEM] * 7,
        )
        core_x = swap(terms[3], "ctx", 1)
        core_own = swap(terms[2], "ctx", 1)
        (sum_x,) = add([terms[1]], [core_x], 1)
        x_own = swap(after(sum_x, rets[-1]) if rets else sum_x, "ctx", 2)
        rets.append(x_own)
        (sum_own,) = add([terms[0]], [core_own], 1)
        final = add([sum_own], [x_own], len(group))
        earlier = [sum_x, sum_own] + (waiting or [])
        waiting = list(final)
        for k, value in zip(group, final):
            if small:
                returned[k] = swap(value, "exp", k) if k else value
            else:
                returned[k] = lax.all_to_all(
                    value, "exp", split_axis=0, concat_axis=0, tiled=True
                )
    (expert_mix,) = call(
        functools.partial(combine_kernel, blocks),
        [shape(rows, features)],
        [pltpu.VMEM((lines, features), BF16)],
        4 * rows * features * lines,
        [route, *[returned[k] for k in range(blocks)]],
        [VMEM] * (1 + blocks),
    )
    return (attention_out.reshape(tokens.shape), expert_mix.reshape(tokens.shape))


def solution(mesh):
    in_specs = (
        P("exp", "ctx", None),
        P("exp", "ctx", None),
        P(),
        P("exp", None),
        P("exp", None),
        P("exp", None),
        P(),
        P(),
        P("exp", None, "ctx"),
        P("exp", None, "ctx"),
        P("exp", "ctx", None),
    )
    out_specs = (P("exp", "ctx", None), P("exp", "ctx", None))
    return jax.shard_map(body, mesh=mesh, in_specs=in_specs, out_specs=out_specs, check_vma=False)
```
